256 devices in a mesh: section: 16 (over y, x_lo, core), dp: 16 (over z, x_hi).
Axes of the slice: x: 4 (x_hi: 2, x_lo: 2; x = x_hi * 2 + x_lo), y: 4, z: 8, core: 2. Of those that a mesh axis runs over, the one named last changes fastest.
Arguments:
- feed: bfloat16 [2, 4, 256, 512], P(None, None, 'dp'), may hold values from -6 to 6
- proj_in: bfloat16 [2, 16, 512, 1536], P(None, 'section'), may hold values from -0.25 to 0.25
- proj_out: bfloat16 [2, 16, 1536, 512], P(None, 'section'), may hold values from -0.15625 to 0.15625
Outputs:
- grad_a: float32 [16, 512, 1536], P('section', 'dp')
- grad_b: float32 [16, 1536, 512], P('section', 'dp')
The draws below stay inside these ranges and needn't reach their ends.
All inputs are finite; a program needn't handle non-finite values.
Results may differ from the reference program's by a relative error of at most 0.023.
Values may be sent and summed in bfloat16 or wider, within the bound.
No kernel may reach another device: no remote copies, remote signals or barrier semaphores. Data moves between devices by JAX's collectives and lax.ppermute only.
A program may use at most 64 MiB of HBM per device.

```python
import jax
import jax.numpy as jnp
from jax import lax

D = 512
R = 1536
MB = 4
TOKENS = 256
N_SECTION = 16


def block_scale(own_key, extent, shards, low, top_value):
    loudness, own = 1.0, jax.random.fold_in(own_key, 6)
    for dim, parts in shards:
        draws = jnp.exp(jax.random.uniform(jax.random.fold_in(own, dim), (parts,), jnp.float32, low / len(shards), top_value / len(shards)))
        loudness = loudness * jnp.repeat(draws, extent[dim] // parts).reshape([-1 if axis == dim else 1 for axis in range(len(extent))])
    return loudness


def scatter_about(rng, shape, spread, limit, cuts=(), dtype=jnp.bfloat16):
    gain = block_scale(rng, shape, cuts, -0.22, 0.18) if cuts else 1.0
    drawn = jax.random.normal(rng, shape, jnp.float32) * spread * gain
    return jnp.minimum(jnp.maximum(drawn, -limit), limit).astype(dtype)


def setup_inputs(seed: int = 0) -> dict:
    key_of = jax.random.split(jax.random.key(seed), 4)
    feed = scatter_about(key_of[0], (2, MB, TOKENS, D), 1.0, 6.0, ((2, 16),))
    proj_in = scatter_about(key_of[1], (2, N_SECTION, D, R), D ** -0.5, 0.25, ((1, 16),))
    proj_out = scatter_about(key_of[2], (2, N_SECTION, R, D), R ** -0.5, 0.15625, ((1, 16),))
    return {"feed": feed, "proj_in": proj_in, "proj_out": proj_out}


def forward_section(activ, weight_in, weight_out):
    wide = activ.astype(jnp.float32)
    factor = lax.rsqrt(lax.optimization_barrier(jnp.mean(wide * wide, axis=-1, keepdims=True)) + 1e-05)
    normed = (wide * factor).astype(jnp.bfloat16)
    before = jnp.dot(normed, weight_in, preferred_element_type=jnp.float32)
    hidden = (before * jax.nn.sigmoid(before)).astype(jnp.bfloat16)
    result = (wide + jnp.dot(hidden, weight_out, preferred_element_type=jnp.float32)).astype(jnp.bfloat16)
    return (result, before)

def backward_section(activ, before, weight_in, weight_out, incoming):
    wide = activ.astype(jnp.float32)
    factor = lax.rsqrt(lax.optimization_barrier(jnp.mean(wide * wide, axis=-1, keepdims=True)) + 1e-05)
    scaled = wide * factor
    normed = scaled.astype(jnp.bfloat16)
    hidden = (before * jax.nn.sigmoid(before)).astype(jnp.bfloat16)
    d_hidden = jnp.dot(incoming, weight_out.T, preferred_element_type=jnp.float32)
    sigma = jax.nn.sigmoid(before)
    d_before = (d_hidden * sigma * (1.0 + before * (1.0 - sigma))).astype(jnp.bfloat16)
    d_normed = jnp.dot(d_before, weight_in.T, preferred_element_type=jnp.float32)
    outgoing = incoming.astype(jnp.float32) + factor * (d_normed - scaled * lax.optimization_barrier(jnp.mean(d_normed * scaled, axis=-1, keepdims=True)))
    grad_in_t = jnp.dot(d_before.T, normed, preferred_element_type=jnp.float32)
    grad_out = jnp.dot(hidden.T, incoming, preferred_element_type=jnp.float32)
    return (outgoing.astype(jnp.bfloat16), grad_in_t, grad_out)

def reference(feed, proj_in, proj_out):
    seed_scale = 8.0 / (MB * TOKENS)
    acc_in = [jnp.zeros((R, D), jnp.float32) for section_index in range(N_SECTION)]
    acc_out = [jnp.zeros((R, D), jnp.float32) for section_index in range(N_SECTION)]
    for relay in range(2):
        for micro_index in range(MB):
            activ = feed[relay, micro_index]
            saved = []
            for section_index in range(N_SECTION):
                holder = section_index if relay == 0 else N_SECTION - 1 - section_index
                result, before = forward_section(activ, proj_in[relay, holder], proj_out[relay, holder])
                saved.append((activ, before))
                activ = result
            incoming = (seed_scale * activ.astype(jnp.float32)).astype(jnp.bfloat16)
            for section_index in range(N_SECTION - 1, -1, -1):
                holder = section_index if relay == 0 else N_SECTION - 1 - section_index
                kept, before = saved[section_index]
                incoming, term_in, term_out = backward_section(kept, before, proj_in[relay, holder], proj_out[relay, holder], incoming)
                acc_in[section_index] = acc_in[section_index] + term_in
                acc_out[section_index] = acc_out[section_index] + term_out
    grad_a = jnp.stack([jnp.transpose(term) for term in acc_in])
    grad_b = jnp.stack(acc_out)
    return (grad_a, grad_b)
```

```python
import functools

import jax
import jax.numpy as jnp
from jax import lax
from jax.experimental import pallas as pl
from jax.experimental.pallas import tpu as pltpu
from jax.sharding import PartitionSpec as P

F32 = jnp.float32
BF16 = jnp.bfloat16
SEED_SCALE = 8.0 / 1024.0
MIB = 1024 * 1024
VMEM = pl.BlockSpec(memory_space=pltpu.VMEM)
SMEM = pl.BlockSpec(memory_space=pltpu.SMEM)
HBM = pl.BlockSpec(memory_space=pltpu.HBM)


def dot(a, b):
    return jnp.dot(a, b, preferred_element_type=F32)


def dot_t(a, b):
    return lax.dot_general(a, b, (((1,), (1,)), ((), ())), preferred_element_type=F32)


def dot_tn(a, b):
    return lax.dot_general(a, b, (((0,), (0,)), ((), ())), preferred_element_type=F32)


def rows_norm(x):
    wide = x.astype(F32)
    factor = lax.rsqrt(jnp.mean(wide * wide, axis=-1, keepdims=True) + 1e-05)
    return wide, factor, wide * factor


def section_forward(x, a, b):
    wide, factor, scaled = rows_norm(x)
    pre = dot(scaled.astype(BF16), a)
    hidden = (pre * jax.nn.sigmoid(pre)).astype(BF16)
    return (wide + dot(hidden, b)).astype(BF16), pre


def section_backward(x, pre, a, b, g):
    wide, factor, scaled = rows_norm(x)
    sigma = jax.nn.sigmoid(pre)
    d_hidden = dot_t(g, b)
    d_pre = (d_hidden * sigma * (1.0 + pre * (1.0 - sigma))).astype(BF16)
    d_normed = dot_t(d_pre, a)
    inner = jnp.mean(d_normed * scaled, axis=-1, keepdims=True)
    return (g.astype(F32) + factor * (d_normed - scaled * inner)).astype(BF16)


def forward_kernel(t, place, x, a0, b0, a1, b1, y):
    @pl.when(place[0] == t)
    def _():
        mid, _ = section_forward(x[...], a0[...], b0[...])
        y[...] = section_forward(mid, a1[...], b1[...])[0]


def turn_kernel(place, *refs):
    n = len(refs) - 11
    xs = refs[:n]
    a0, b0, a1, b1, x, x_sent, mid, pre0, pre1, seed, g_out = refs[n:]
    for t in range(n):

        @pl.when(place[0] == t)
        def _():
            x[...] = xs[t][...]
            x_sent[...] = xs[t][...]

    h, p0 = section_forward(x[...], a0[...], b0[...])
    mid[...] = h
    pre0[...] = p0
    y, p1 = section_forward(h, a1[...], b1[...])
    pre1[...] = p1

    @pl.when(place[0] == n - 1)
    def _():
        g = (SEED_SCALE * y.astype(F32)).astype(BF16)
        seed[...] = g
        half = section_backward(h, p1, a1[...], b1[...], g)
        g_out[...] = section_backward(x[...], p0, a0[...], b0[...], half)


def backward_kernel(t, place, g, x, mid, pre0, pre1, a0, b0, a1, b1, g_out):
    @pl.when(place[0] == t)
    def _():
        half = section_backward(mid[...], pre1[...], a1[...], b1[...], g[...])
        g_out[...] = section_backward(x[...], pre0[...], a0[...], b0[...], half)


def choose_kernel(place, *refs):
    gs, g = refs[:-1], refs[-1]
    for t, ref in enumerate(gs):

        @pl.when(place[0] == t)
        def _():
            g[...] = ref[...]


def follow_kernel(n, *refs):
    del n, refs


def load_kernel(place, feed, proj_in, proj_out, x0, a0, b0, a_send, b_send, sems):
    own, other = place[2], 1 - place[2]
    moves = (
        (proj_in.at[other, 0], a_send),
        (proj_out.at[other, 0], b_send),
        (feed.at[own], x0),
        (proj_in.at[own, 0], a0),
        (proj_out.at[own, 0], b0),
    )
    copies = [pltpu.make_async_copy(s, t, sems.at[i]) for i, (s, t) in enumerate(moves)]
    for copy in copies:
        copy.start()
    for copy in copies:
        copy.wait()


def land_kernel(a_ref, b_ref, a1, b1, sems):
    copies = [
        pltpu.make_async_copy(a_ref, a1, sems.at[0]),
        pltpu.make_async_copy(b_ref, b1, sems.at[1]),
    ]
    for copy in copies:
        copy.start()
    for copy in copies:
        copy.wait()


def columns_of(replica):
    a_col = pl.multiple_of((replica // 4) * 128, 128)
    b_col = pl.multiple_of(jnp.minimum((replica * 96) // 128, 10) * 128, 128)
    return a_col, b_col


def collect(pieces, whole, sems):
    start, copies = 0, []
    for i, piece in enumerate(pieces):
        count = piece.shape[0]
        copies.append(
            pltpu.make_async_copy(piece, whole.at[pl.ds(start, count), :], sems.at[i])
        )
        start += count
    for copy in copies:
        copy.start()
    for copy in copies:
        copy.wait()


def recompute_kernel(n_pieces, chunk, place, *refs):
    xs = refs[:n_pieces]
    a0, b0, a1, b1, mids, slope0, slope1, nrm0, nrm1, hid0, hid1 = refs[n_pieces : n_pieces + 11]
    x_all, wide_n, wide_h, sems = refs[n_pieces + 11 :]
    collect(xs, x_all, sems)
    a_col, b_col = columns_of(place[1])

    def section(x, a, b, part, slope, nrm, hid):
        wide, factor, scaled = rows_norm(x)
        normed = scaled.astype(BF16)
        wide_n[...] = normed
        pre = dot(normed, a[...])
        sigma = jax.nn.sigmoid(pre)
        hidden = (pre * sigma).astype(BF16)
        wide_h[...] = hidden
        slope[part, :] = (sigma * (1.0 + pre * (1.0 - sigma))).astype(slope.dtype)
        nrm[part, :] = wide_n[:, pl.ds(a_col, 128)]
        hid[part, :] = wide_h[:, pl.ds(b_col, 256)]
        if b is None:
            return None
        return (wide + dot(hidden, b[...])).astype(BF16)

    @pl.loop(0, x_all.shape[0] // chunk)
    def _(i):
        part = pl.ds(pl.multiple_of(i * chunk, chunk), chunk)
        mid = section(x_all[part, :], a0, b0, part, slope0, nrm0, hid0)
        mids[part, :] = mid
        section(mid, a1, None, part, slope1, nrm1, hid1)


def grad_kernel(n_pieces, chunk, place, *refs):
    gs = refs[:n_pieces]
    mids, slope0, slope1, nrm0, nrm1, hid0, hid1, a0, b0, a1, b1 = refs[n_pieces : n_pieces + 11]
    leave, stay = refs[n_pieces + 11 : n_pieces + 13]
    g_all, acc_a0, acc_b0, acc_a1, acc_b1, sems = refs[n_pieces + 13 :]
    collect(gs, g_all, sems)
    replica, core = place[1], place[2]
    a_col, b_col = columns_of(replica)

    @pl.loop(0, g_all.shape[0] // chunk)
    def _(i):
        part = pl.ds(pl.multiple_of(i * chunk, chunk), chunk)
        g1 = g_all[part, :]
        wide1, factor1, scaled1 = rows_norm(mids[part, :])
        d_pre1 = (dot_t(g1, b1[...]) * slope1[part, :].astype(F32)).astype(BF16)
        d_normed1 = dot_t(d_pre1, a1[...])
        inner = jnp.mean(d_normed1 * scaled1, axis=-1, keepdims=True)
        g0 = (g1.astype(F32) + factor1 * (d_normed1 - scaled1 * inner)).astype(BF16)
        d_pre0 = (dot_t(g0, b0[...]) * slope0[part, :].astype(F32)).astype(BF16)
        terms = (
            (acc_a0, dot_tn(nrm0[part, :], d_pre0)),
            (acc_a1, dot_tn(nrm1[part, :], d_pre1)),
            (acc_b0, dot_tn(hid0[part, :], g0)),
            (acc_b1, dot_tn(hid1[part, :], g1)),
        )
        for acc, term in terms:
            acc[...] = jnp.where(i == 0, term, acc[...] + term)

    a_row = pl.multiple_of(lax.rem(replica, 4) * 32, 32)
    b_row = pl.multiple_of(replica * 96 - b_col, 32)
    d = g_all.shape[1]

    def write(target, acc_a, acc_b):
        count = acc_a.shape[1] // d
        for j in range(count):
            target[32 * j : 32 * (j + 1), :] = acc_a[
                pl.ds(a_row, 32), d * j : d * (j + 1)
            ].astype(target.dtype)
        target[32 * count : 32 * count + 96, :] = acc_b[pl.ds(b_row, 96), :].astype(target.dtype)

    @pl.when(core == 0)
    def _():
        write(stay, acc_a0, acc_b0)
        write(leave, acc_a1, acc_b1)

    @pl.when(core == 1)
    def _():
        write(leave, acc_a0, acc_b0)
        write(stay, acc_a1, acc_b1)


def finish_kernel(place, stay, first, second, grad_a, grad_b):
    own = jnp.where(place[2] == 0, stay[...].astype(F32), second[...].astype(F32))
    total = own + first[...].astype(F32)
    d = total.shape[1]
    count = grad_a.shape[1] // d
    for j in range(count):
        grad_a[:, d * j : d * (j + 1)] = total[32 * j : 32 * (j + 1), :]
    grad_b[...] = total[32 * count :, :]


def call(kernel, ins, outs, flops, scratch=(), limit=8, out_specs=None, aliases=None):
    return pl.pallas_call(
        kernel,
        out_shape=outs,
        in_specs=ins,
        out_specs=jax.tree.map(lambda _: VMEM, outs) if out_specs is None else out_specs,
        scratch_shapes=list(scratch),
        input_output_aliases=aliases or {},
        compiler_params=pltpu.CompilerParams(vmem_limit_bytes=limit * MIB),
        cost_estimate=pl.CostEstimate(flops=flops, bytes_accessed=MIB, transcendentals=0),
    )


class Gather:
    def __init__(self, x):
        self.last = [x]
        self.pieces = [x]
        self.steps = 1 + lax.axis_size("dp") // 4
        self.taken = 0

    def step(self):
        n = lax.axis_size("dp")
        up = [(d, (d + 2) % n) for d in range(n)]
        down = [(d, (d - 2) % n) for d in range(n)]
        cross = [(d, d ^ 1) for d in range(n)]
        if self.taken == 0:
            sends = [(self.last[0], cross)]
        elif self.taken == 1:
            sends = [(v, p) for p in (up, down) for v in self.last]
        elif self.taken == self.steps - 1:
            sends = [(self.last[0], up), (self.last[3], down)]
        else:
            sends = list(zip(self.last, (up, up, down, down)))
        got = [lax.ppermute(v, "dp", p) for v, p in sends]
        self.pieces += got
        self.last = self.last + got if self.taken == 0 else got
        self.taken += 1

    def follow(self, value):
        shapes = [jax.ShapeDtypeStruct(v.shape, v.dtype) for v in self.last]
        n = len(shapes)
        self.last = list(
            call(
                functools.partial(follow_kernel, n),
                [VMEM] * (n + 1),
                shapes,
                FOLLOW_FLOPS,
                aliases={i: i for i in range(n)},
                limit=1,
            )(*self.last, value)
        )


FOLLOW_FLOPS = 4 * 10**9


def per_device(feed, proj_in, proj_out):
    sections = lax.axis_size("section")
    stages = sections // 2
    replicas = lax.axis_size("dp")
    position = lax.axis_index("section")
    replica = lax.axis_index("dp")
    core = lax.rem(position, 2)
    chip = lax.div(position, 2)
    stage = jnp.where(core == 0, chip, stages - 1 - chip)
    place = jnp.stack([stage, replica, core]).astype(jnp.int32)

    d, r = proj_in.shape[2:]
    micro, part = feed.shape[1:3]
    rows = micro * part
    total = rows * replicas
    chunk = 256

    def bf(*shape):
        return jax.ShapeDtypeStruct(shape, BF16)

    def f32(*shape):
        return jax.ShapeDtypeStruct(shape, F32)

    place, feed, proj_in, proj_out = lax.optimization_barrier((place, feed, proj_in, proj_out))
    feed, proj_in, proj_out = (
        pltpu.with_memory_space_constraint(v, pltpu.HBM) for v in (feed, proj_in, proj_out)
    )
    x0, a0, b0, a_send, b_send = call(
        load_kernel,
        [SMEM, HBM, HBM, HBM],
        (bf(micro, part, d), bf(d, r), bf(r, d), bf(d, r), bf(r, d)),
        0,
        scratch=(pltpu.SemaphoreType.DMA((5,)),),
        out_specs=(VMEM, VMEM, VMEM, HBM, HBM),
    )(place, feed, proj_in, proj_out)
    swap = [(s, s ^ 1) for s in range(sections)]
    a1 = lax.ppermute(a_send, "section", swap)
    b1 = lax.ppermute(b_send, "section", swap)
    a1, b1 = call(
        land_kernel,
        [HBM, HBM],
        (bf(d, r), bf(r, d)),
        0,
        scratch=(pltpu.SemaphoreType.DMA((2,)),),
    )(a1, b1)
    weights = (a0, b0, a1, b1)
    step_flops = 8 * rows * d * r

    def hop(value, t, back=False):
        last = sections - 1
        pairs = [(2 * t, 2 * t + 2), (last - 2 * t, last - 2 * t - 2)]
        return lax.ppermute(value, "section", [(b, a) for a, b in pairs] if back else pairs)

    xs = [x0.reshape(rows, d)]
    for t in range(stages - 1):
        y = call(
            functools.partial(forward_kernel, t), [SMEM] + [VMEM] * 5, bf(rows, d), step_flops
        )(place, xs[-1], *weights)
        xs.append(hop(y, t))
    x, x_sent, mid, pre0, pre1, seed, back = call(
        turn_kernel,
        [SMEM] + [VMEM] * (stages + 4),
        (bf(rows, d),) * 3 + (f32(rows, r),) * 2 + (bf(rows, d),) * 2,
        2 * step_flops,
    )(place, *xs, *weights)

    gather = Gather(x_sent)
    gs = [seed]
    kept = None
    for t in range(stages - 2, -1, -1):
        came = hop(back, t, True)
        if gather.taken < gather.steps:
            gather.follow(back)
            gather.step()
        elif kept is None:
            pieces = gather.pieces
            kept = call(
                functools.partial(recompute_kernel, len(pieces), chunk),
                [SMEM] + [HBM] * len(pieces) + [VMEM] * 4,
                (
                    bf(total, d),
                    bf(total, r),
                    bf(total, r),
                    bf(total, 128),
                    bf(total, 128),
                    bf(total, 256),
                    bf(total, 256),
                ),
                6 * total * d * r,
                scratch=(
                    pltpu.VMEM((total, d), BF16),
                    pltpu.VMEM((chunk, d), BF16),
                    pltpu.VMEM((chunk, r), BF16),
                    pltpu.SemaphoreType.DMA((len(pieces),)),
                ),
                limit=20,
            )(place, *pieces, *weights)
            came, kept = lax.optimization_barrier((came, kept))
        gs.append(came)
        if t > 0:
            back = call(
                functools.partial(backward_kernel, t),
                [SMEM] + [VMEM] * 9,
                bf(rows, d),
                step_flops,
            )(place, came, x, mid, pre0, pre1, *weights)
    g = call(choose_kernel, [SMEM] + [VMEM] * stages, bf(rows, d), 0)(place, *gs[::-1])
    gather = Gather(g)
    for _ in range(gather.steps):
        gather.step()
    pieces = gather.pieces

    slab = (d * r + r * d) // replicas // d
    leave, stay = call(
        functools.partial(grad_kernel, len(pieces), chunk),
        [SMEM] + [HBM] * len(pieces) + [VMEM] * 11,
        (bf(slab, d), bf(slab, d)),
        10 * total * d * r,
        scratch=(
            pltpu.VMEM((total, d), BF16),
            pltpu.VMEM((128, r), F32),
            pltpu.VMEM((256, d), F32),
            pltpu.VMEM((128, r), F32),
            pltpu.VMEM((256, d), F32),
            pltpu.SemaphoreType.DMA((len(pieces),)),
        ),
        limit=20,
    )(place, *pieces, *kept, *weights)
    cross = [(s, s + 1 if s % 2 == 0 else sections - 1 - s) for s in range(sections)]
    mirror = [(s, sections - s) for s in range(1, sections, 2)]
    mirror += [(s, s) for s in range(0, sections, 2)]
    first = lax.ppermute(leave, "section", cross)
    second = lax.ppermute(stay, "section", mirror)
    grad_a, grad_b = call(
        finish_kernel, [SMEM] + [VMEM] * 3, (f32(d // replicas, r), f32(r // replicas, d)), 0
    )(place, stay, first, second)
    return grad_a[None], grad_b[None]


def solution(mesh):
    in_specs = (
        P(None, None, "dp", None),
        P(None, "section", None, None),
        P(None, "section", None, None),
    )
    out_specs = (P("section", "dp", None), P("section", "dp", None))
    return jax.shard_map(
        per_device, mesh=mesh, in_specs=in_specs, out_specs=out_specs, check_vma=False
    )
```

```python
import functools

import jax
import jax.numpy as jnp
from jax import lax
from jax.experimental import pallas as pl
from jax.experimental.pallas import tpu as pltpu
from jax.sharding import PartitionSpec as P

F32 = jnp.float32
BF16 = jnp.bfloat16
SEED_SCALE = 8.0 / 1024.0
MIB = 1024 * 1024
VMEM = pl.BlockSpec(memory_space=pltpu.VMEM)
SMEM = pl.BlockSpec(memory_space=pltpu.SMEM)
HBM = pl.BlockSpec(memory_space=pltpu.HBM)


def dot(a, b):
    return jnp.dot(a, b, preferred_element_type=F32)


def dot_t(a, b):
    return lax.dot_general(a, b, (((1,), (1,)), ((), ())), preferred_element_type=F32)


def dot_tn(a, b):
    return lax.dot_general(a, b, (((0,), (0,)), ((), ())), preferred_element_type=F32)


def rows_norm(x):
    wide = x.astype(F32)
    factor = lax.rsqrt(jnp.mean(wide * wide, axis=-1, keepdims=True) + 1e-05)
    return wide, factor, wide * factor


def section_forward(x, a, b):
    wide, factor, scaled = rows_norm(x)
    pre = dot(scaled.astype(BF16), a)
    hidden = (pre * jax.nn.sigmoid(pre)).astype(BF16)
    return (wide + dot(hidden, b)).astype(BF16), pre


def section_backward(x, pre, a, b, g):
    wide, factor, scaled = rows_norm(x)
    sigma = jax.nn.sigmoid(pre)
    d_hidden = dot_t(g, b)
    d_pre = (d_hidden * sigma * (1.0 + pre * (1.0 - sigma))).astype(BF16)
    d_normed = dot_t(d_pre, a)
    inner = jnp.mean(d_normed * scaled, axis=-1, keepdims=True)
    return (g.astype(F32) + factor * (d_normed - scaled * inner)).astype(BF16)


def forward_kernel(t, place, x, a0, b0, a1, b1, y):
    @pl.when(place[0] == t)
    def _():
        mid, _ = section_forward(x[...], a0[...], b0[...])
        y[...] = section_forward(mid, a1[...], b1[...])[0]


def turn_kernel(place, *refs):
    n = len(refs) - 11
    xs = refs[:n]
    a0, b0, a1, b1, x, x_sent, mid, pre0, pre1, seed, g_out = refs[n:]
    for t in range(n):

        @pl.when(place[0] == t)
        def _():
            x[...] = xs[t][...]
            x_sent[...] = xs[t][...]

    h, p0 = section_forward(x[...], a0[...], b0[...])
    mid[...] = h
    pre0[...] = p0
    y, p1 = section_forward(h, a1[...], b1[...])
    pre1[...] = p1

    @pl.when(place[0] == n - 1)
    def _():
        g = (SEED_SCALE * y.astype(F32)).astype(BF16)
        seed[...] = g
        half = section_backward(h, p1, a1[...], b1[...], g)
        g_out[...] = section_backward(x[...], p0, a0[...], b0[...], half)


def backward_kernel(t, place, g, x, mid, pre0, pre1, a0, b0, a1, b1, g_out):
    @pl.when(place[0] == t)
    def _():
        half = section_backward(mid[...], pre1[...], a1[...], b1[...], g[...])
        g_out[...] = section_backward(x[...], pre0[...], a0[...], b0[...], half)


def choose_kernel(place, *refs):
    gs, g = refs[:-1], refs[-1]
    for t, ref in enumerate(gs):

        @pl.when(place[0] == t)
        def _():
            g[...] = ref[...]


def follow_kernel(n, *refs):
    del n, refs


def load_kernel(place, feed, proj_in, proj_out, x0, a0, b0, a_send, b_send, sems):
    own, other = place[2], 1 - place[2]
    moves = (
        (proj_in.at[other, 0], a_send),
        (proj_out.at[other, 0], b_send),
        (feed.at[own], x0),
        (proj_in.at[own, 0], a0),
        (proj_out.at[own, 0], b0),
    )
    copies = [pltpu.make_async_copy(s, t, sems.at[i]) for i, (s, t) in enumerate(moves)]
    for copy in copies:
        copy.start()
    for copy in copies:
        copy.wait()


def land_kernel(a_ref, b_ref, a1, b1, sems):
    copies = [
        pltpu.make_async_copy(a_ref, a1, sems.at[0]),
        pltpu.make_async_copy(b_ref, b1, sems.at[1]),
    ]
    for copy in copies:
        copy.start()
    for copy in copies:
        copy.wait()


def columns_of(replica):
    pair = replica // 2
    a_col = pl.multiple_of((pair // 2) * 128, 128)
    b_col = pl.multiple_of(((pair * 192) // 128) * 128, 128)
    return a_col, b_col


def collect(pieces, whole, sems):
    start, copies = 0, []
    for i, piece in enumerate(pieces):
        count = piece.shape[0]
        copies.append(
            pltpu.make_async_copy(piece, whole.at[pl.ds(start, count), :], sems.at[i])
        )
        start += count
    for copy in copies:
        copy.start()
    for copy in copies:
        copy.wait()


def recompute_kernel(n_pieces, chunk, place, *refs):
    xs = refs[:n_pieces]
    a0, b0, a1, b1, mids, slope0, slope1, nrm0, nrm1, hid0, hid1 = refs[n_pieces : n_pieces + 11]
    x_all, wide_n, wide_h, sems = refs[n_pieces + 11 :]
    collect(xs, x_all, sems)
    a_col, b_col = columns_of(place[1])

    def section(x, a, b, part, slope, nrm, hid):
        wide, factor, scaled = rows_norm(x)
        normed = scaled.astype(BF16)
        wide_n[...] = normed
        pre = dot(normed, a[...])
        sigma = jax.nn.sigmoid(pre)
        hidden = (pre * sigma).astype(BF16)
        wide_h[...] = hidden
        slope[part, :] = (sigma * (1.0 + pre * (1.0 - sigma))).astype(slope.dtype)
        nrm[part, :] = wide_n[:, pl.ds(a_col, 128)]
        hid[part, :] = wide_h[:, pl.ds(b_col, 256)]
        if b is None:
            return None
        return (wide + dot(hidden, b[...])).astype(BF16)

    @pl.loop(0, x_all.shape[0] // chunk)
    def _(i):
        part = pl.ds(pl.multiple_of(i * chunk, chunk), chunk)
        mid = section(x_all[part, :], a0, b0, part, slope0, nrm0, hid0)
        mids[part, :] = mid
        section(mid, a1, None, part, slope1, nrm1, hid1)


def grad_kernel(n_pieces, chunk, place, *refs):
    gs = refs[:n_pieces]
    mids, slope0, slope1, nrm0, nrm1, hid0, hid1, a0, b0, a1, b1 = refs[n_pieces : n_pieces + 11]
    leave, stay, leave_near, stay_near = refs[n_pieces + 11 : n_pieces + 15]
    g_all, acc_a0, acc_b0, acc_a1, acc_b1, sems = refs[n_pieces + 15 :]
    collect(gs, g_all, sems)
    replica, core = place[1], place[2]
    a_col, b_col = columns_of(replica)

    @pl.loop(0, g_all.shape[0] // chunk)
    def _(i):
        part = pl.ds(pl.multiple_of(i * chunk, chunk), chunk)
        g1 = g_all[part, :]
        wide1, factor1, scaled1 = rows_norm(mids[part, :])
        d_pre1 = (dot_t(g1, b1[...]) * slope1[part, :].astype(F32)).astype(BF16)
        d_normed1 = dot_t(d_pre1, a1[...])
        inner = jnp.mean(d_normed1 * scaled1, axis=-1, keepdims=True)
        g0 = (g1.astype(F32) + factor1 * (d_normed1 - scaled1 * inner)).astype(BF16)
        d_pre0 = (dot_t(g0, b0[...]) * slope0[part, :].astype(F32)).astype(BF16)
        terms = (
            (acc_a0, dot_tn(nrm0[part, :], d_pre0)),
            (acc_a1, dot_tn(nrm1[part, :], d_pre1)),
            (acc_b0, dot_tn(hid0[part, :], g0)),
            (acc_b1, dot_tn(hid1[part, :], g1)),
        )
        for acc, term in terms:
            acc[...] = jnp.where(i == 0, term, acc[...] + term)

    d = g_all.shape[1]

    def write(target, acc_a, acc_b, slice_of):
        a_row = pl.multiple_of(lax.rem(slice_of, 4) * 32, 32)
        b_row = pl.multiple_of(slice_of * 96 - b_col, 32)
        count = acc_a.shape[1] // d
        for j in range(count):
            target[32 * j : 32 * (j + 1), :] = acc_a[
                pl.ds(a_row, 32), d * j : d * (j + 1)
            ].astype(target.dtype)
        target[32 * count : 32 * count + 96, :] = acc_b[pl.ds(b_row, 96), :].astype(target.dtype)

    near = replica + 1 - 2 * lax.rem(replica, 2)

    @pl.when(core == 0)
    def _():
        write(stay, acc_a0, acc_b0, replica)
        write(leave, acc_a1, acc_b1, replica)
        write(stay_near, acc_a0, acc_b0, near)
        write(leave_near, acc_a1, acc_b1, near)

    @pl.when(core == 1)
    def _():
        write(leave, acc_a0, acc_b0, replica)
        write(stay, acc_a1, acc_b1, replica)
        write(leave_near, acc_a0, acc_b0, near)
        write(stay_near, acc_a1, acc_b1, near)


def finish_kernel(first, second, third, fourth, grad_a, grad_b):
    total = first[...].astype(F32) + second[...].astype(F32)
    total = total + (third[...].astype(F32) + fourth[...].astype(F32))
    d = total.shape[1]
    count = grad_a.shape[1] // d
    for j in range(count):
        grad_a[:, d * j : d * (j + 1)] = total[32 * j : 32 * (j + 1), :]
    grad_b[...] = total[32 * count :, :]


def call(kernel, ins, outs, flops, scratch=(), limit=8, out_specs=None, aliases=None):
    return pl.pallas_call(
        kernel,
        out_shape=outs,
        in_specs=ins,
        out_specs=jax.tree.map(lambda _: VMEM, outs) if out_specs is None else out_specs,
        scratch_shapes=list(scratch),
        input_output_aliases=aliases or {},
        compiler_params=pltpu.CompilerParams(vmem_limit_bytes=limit * MIB),
        cost_estimate=pl.CostEstimate(flops=flops, bytes_accessed=MIB, transcendentals=0),
    )


def along(values, steps):
    n = lax.axis_size("dp")
    return [
        lax.ppermute(v, "dp", [(d, (d + 2 * k) % n) for d in range(n)])
        for v, k in zip(values, steps)
    ]


def gather_near(x):
    return along([x] * 4, (1, -1, 2, -2))


def gather_far(low, high):
    return along([low, high, low], (1, -1, 2))


def follow(arrays, value):
    shapes = [jax.ShapeDtypeStruct(v.shape, v.dtype) for v in arrays]
    n = len(shapes)
    return call(
        functools.partial(follow_kernel, n),
        [VMEM] * (n + 1),
        shapes,
        FOLLOW_FLOPS,
        aliases={i: i for i in range(n)},
        limit=1,
    )(*arrays, value)


FOLLOW_FLOPS = 4 * 10**9


def per_device(feed, proj_in, proj_out):
    sections = lax.axis_size("section")
    stages = sections // 2
    replicas = lax.axis_size("dp")
    position = lax.axis_index("section")
    replica = lax.axis_index("dp")
    core = lax.rem(position, 2)
    chip = lax.div(position, 2)
    stage = jnp.where(core == 0, chip, stages - 1 - chip)
    place = jnp.stack([stage, replica, core]).astype(jnp.int32)

    d, r = proj_in.shape[2:]
    micro, part = feed.shape[1:3]
    rows = micro * part
    total = rows * replicas // 2
    chunk = 256

    def bf(*shape):
        return jax.ShapeDtypeStruct(shape, BF16)

    def f32(*shape):
        return jax.ShapeDtypeStruct(shape, F32)

    place, feed, proj_in, proj_out = lax.optimization_barrier((place, feed, proj_in, proj_out))
    feed, proj_in, proj_out = (
        pltpu.with_memory_space_constraint(v, pltpu.HBM) for v in (feed, proj_in, proj_out)
    )
    x0, a0, b0, a_send, b_send = call(
        load_kernel,
        [SMEM, HBM, HBM, HBM],
        (bf(micro, part, d), bf(d, r), bf(r, d), bf(d, r), bf(r, d)),
        0,
        scratch=(pltpu.SemaphoreType.DMA((5,)),),
        out_specs=(VMEM, VMEM, VMEM, HBM, HBM),
    )(place, feed, proj_in, proj_out)
    swap = [(s, s ^ 1) for s in range(sections)]
    a1 = lax.ppermute(a_send, "section", swap)
    b1 = lax.ppermute(b_send, "section", swap)
    a1, b1 = call(
        land_kernel,
        [HBM, HBM],
        (bf(d, r), bf(r, d)),
        0,
        scratch=(pltpu.SemaphoreType.DMA((2,)),),
    )(a1, b1)
    weights = (a0, b0, a1, b1)
    step_flops = 8 * rows * d * r

    def hop(value, t, back=False, closed=True):
        last = sections - 1
        pairs = [(2 * t, 2 * t + 2), (last - 2 * t, last - 2 * t - 2)]
        if back:
            pairs = [(b, a) for a, b in pairs]
        if closed:
            cycles = []
            for a, b in pairs:
                if (a, b) not in cycles:
                    cycles += [(a, b), (b, b ^ 1), (b ^ 1, a ^ 1), (a ^ 1, a)]
            used = [a for a, _ in cycles]
            pairs = cycles + [(s, s ^ 1) for s in range(sections) if s not in used]
        return lax.ppermute(value, "section", pairs)

    xs = [x0.reshape(rows, d)]
    for t in range(stages - 1):
        y = call(
            functools.partial(forward_kernel, t), [SMEM] + [VMEM] * 5, bf(rows, d), step_flops
        )(place, xs[-1], *weights)
        xs.append(hop(y, t))
    x, x_sent, mid, pre0, pre1, seed, back = call(
        turn_kernel,
        [SMEM] + [VMEM] * (stages + 4),
        (bf(rows, d),) * 3 + (f32(rows, r),) * 2 + (bf(rows, d),) * 2,
        2 * step_flops,
    )(place, *xs, *weights)

    gs = [seed]
    pieces, kept = [x], None
    for t in range(stages - 2, -1, -1):
        came = hop(back, t, True, kept is not None)
        if len(pieces) == 1:
            (x_sent,) = follow([x_sent], back)
            pieces += gather_near(x_sent)
        elif len(pieces) == 5:
            pieces += gather_far(*follow(pieces[3:], back))
        elif kept is None:
            kept = call(
                functools.partial(recompute_kernel, len(pieces), chunk),
                [SMEM] + [HBM] * len(pieces) + [VMEM] * 4,
                (
                    bf(total, d),
                    bf(total, r),
                    bf(total, r),
                    bf(total, 128),
                    bf(total, 128),
                    bf(total, 256),
                    bf(total, 256),
                ),
                6 * total * d * r,
                scratch=(
                    pltpu.VMEM((total, d), BF16),
                    pltpu.VMEM((chunk, d), BF16),
                    pltpu.VMEM((chunk, r), BF16),
                    pltpu.SemaphoreType.DMA((len(pieces),)),
                ),
                limit=20,
            )(place, *pieces, *weights)
            came, kept = lax.optimization_barrier((came, kept))
        gs.append(came)
        if t > 0:
            back = call(
                functools.partial(backward_kernel, t),
                [SMEM] + [VMEM] * 9,
                bf(rows, d),
                step_flops,
            )(place, came, x, mid, pre0, pre1, *weights)
    g = call(choose_kernel, [SMEM] + [VMEM] * stages, bf(rows, d), 0)(place, *gs[::-1])
    pieces = [g] + gather_near(g)
    pieces += gather_far(*pieces[3:])

    slab = (d * r + r * d) // replicas // d
    leave, stay, leave_near, stay_near = call(
        functools.partial(grad_kernel, len(pieces), chunk),
        [SMEM] + [HBM] * len(pieces) + [VMEM] * 11,
        (bf(slab, d),) * 4,
        10 * total * d * r,
        scratch=(
            pltpu.VMEM((total, d), BF16),
            pltpu.VMEM((128, r), F32),
            pltpu.VMEM((256, d), F32),
            pltpu.VMEM((128, r), F32),
            pltpu.VMEM((256, d), F32),
            pltpu.SemaphoreType.DMA((len(pieces),)),
        ),
        limit=20,
    )(place, *pieces, *kept, *weights)
    cross = [(s, s + 1 if s % 2 == 0 else sections - 1 - s) for s in range(sections)]
    mirror = [(s, s if s % 2 == 0 else sections - s) for s in range(sections)]

    def send(value, targets, near):
        pairs = [
            (s * replicas + e, t * replicas + (e ^ near)) for s, t in targets for e in range(replicas)
        ]
        return lax.ppermute(value, ("section", "dp"), pairs)

    parts = [
        send(leave_near, cross, 1),
        send(stay_near, mirror, 1),
        send(leave, cross, 0),
        send(stay, mirror, 0),
    ]
    grad_a, grad_b = call(
        finish_kernel, [VMEM] * 4, (f32(d // replicas, r), f32(r // replicas, d)), 0
    )(*parts)
    return grad_a[None], grad_b[None]


def solution(mesh):
    in_specs = (
        P(None, None, "dp", None),
        P(None, "section", None, None),
        P(None, "section", None, None),
    )
    out_specs = (P("section", "dp", None), P("section", "dp", None))
    return jax.shard_map(
        per_device, mesh=mesh, in_specs=in_specs, out_specs=out_specs, check_vma=False
    )
```

```python
import functools

import jax
import jax.numpy as jnp
from jax import lax
from jax.experimental import pallas as pl
from jax.experimental.pallas import tpu as pltpu
from jax.sharding import PartitionSpec as P

F32 = jnp.float32
BF16 = jnp.bfloat16
SEED_SCALE = 8.0 / 1024.0
MIB = 1024 * 1024
VMEM = pl.BlockSpec(memory_space=pltpu.VMEM)
SMEM = pl.BlockSpec(memory_space=pltpu.SMEM)
HBM = pl.BlockSpec(memory_space=pltpu.HBM)


def dot(a, b):
    return jnp.dot(a, b, preferred_element_type=F32)


def dot_tn(a, b):
    return lax.dot_general(a, b, (((0,), (0,)), ((), ())), preferred_element_type=F32)


def rows_norm(x):
    wide = x.astype(F32)
    factor = lax.rsqrt(jnp.mean(wide * wide, axis=-1, keepdims=True) + 1e-05)
    return wide, factor, wide * factor


def section_forward(x, a, b):
    wide, factor, scaled = rows_norm(x)
    pre = dot(scaled.astype(BF16), a)
    hidden = (pre * jax.nn.sigmoid(pre)).astype(BF16)
    return (wide + dot(hidden, b)).astype(BF16), pre


def slope_of(pre):
    sigma = jax.nn.sigmoid(pre)
    return sigma * (1.0 + pre * (1.0 - sigma))


def section_backward(x, slope, a_t, b_t, g):
    wide, factor, scaled = rows_norm(x)
    d_pre = (dot(g, b_t) * slope).astype(BF16)
    d_normed = dot(d_pre, a_t)
    inner = jnp.mean(d_normed * scaled, axis=-1, keepdims=True)
    return (g.astype(F32) + factor * (d_normed - scaled * inner)).astype(BF16)


def forward_kernel(t, place, x, a0, b0, a1, b1, y):
    @pl.when(place[0] == t)
    def _():
        mid, _ = section_forward(x[...], a0[...], b0[...])
        y[...] = section_forward(mid, a1[...], b1[...])[0]


def turn_kernel(place, *refs):
    n = len(refs) - 15
    xs = refs[:n]
    a0, b0, a1, b1, a0t, b0t, a1t, b1t, x, x_sent, mid, slope0, slope1, seed, g_out = refs[n:]
    for t in range(n):

        @pl.when(place[0] == t)
        def _():
            x[...] = xs[t][...]
            x_sent[...] = xs[t][...]

    h, p0 = section_forward(x[...], a0[...], b0[...])
    mid[...] = h
    slope0[...] = slope_of(p0)
    y, p1 = section_forward(h, a1[...], b1[...])
    slope1[...] = slope_of(p1)

    @pl.when(place[0] == n - 1)
    def _():
        g = (SEED_SCALE * y.astype(F32)).astype(BF16)
        seed[...] = g
        half = section_backward(h, slope1[...], a1t[...], b1t[...], g)
        g_out[...] = section_backward(x[...], slope0[...], a0t[...], b0t[...], half)


def backward_kernel(t, place, g, x, mid, slope0, slope1, a0t, b0t, a1t, b1t, g_out):
    @pl.when(place[0] == t)
    def _():
        half = section_backward(mid[...], slope1[...], a1t[...], b1t[...], g[...])
        g_out[...] = section_backward(x[...], slope0[...], a0t[...], b0t[...], half)


def choose_kernel(place, *refs):
    gs, g = refs[:-1], refs[-1]
    for t, ref in enumerate(gs):

        @pl.when(place[0] == t)
        def _():
            g[...] = ref[...]


def follow_kernel(n, *refs):
    del n, refs


def copy_all(moves, sems):
    copies = [pltpu.make_async_copy(s, t, sems.at[i]) for i, (s, t) in enumerate(moves)]
    for copy in copies:
        copy.start()
    for copy in copies:
        copy.wait()


def offer_kernel(place, proj_in, proj_out, a_send, b_send, sems):
    other = 1 - place[2]
    copy_all(((proj_in.at[other, 0], a_send), (proj_out.at[other, 0], b_send)), sems)


def load_kernel(place, feed, proj_in, proj_out, x0, a0, b0, sems):
    own = place[2]
    copy_all(
        ((proj_in.at[own, 0], a0), (proj_out.at[own, 0], b0), (feed.at[own], x0)), sems
    )


def land_kernel(a_ref, b_ref, a1, b1, sems):
    copy_all(((a_ref, a1), (b_ref, b1)), sems)


def turn_weights_kernel(y, *refs):
    del y
    for source, target in zip(refs[:4], refs[4:]):
        step = 256

        @pl.loop(0, source.shape[0] // step)
        def _(i):
            part = pl.ds(pl.multiple_of(i * step, step), step)
            target[:, part] = source[part, :].T


def columns_of(replica):
    pair = replica // 2
    a_col = pl.multiple_of((pair // 2) * 128, 128)
    b_col = pl.multiple_of(((pair * 192) // 128) * 128, 128)
    return a_col, b_col


def collect(pieces, whole, sems):
    start, copies = 0, []
    for i, piece in enumerate(pieces):
        count = piece.shape[0]
        copies.append(
            pltpu.make_async_copy(piece, whole.at[pl.ds(start, count), :], sems.at[i])
        )
        start += count
    for copy in copies:
        copy.start()
    for copy in copies:
        copy.wait()


def recompute_kernel(n_pieces, chunk, place, *refs):
    xs = refs[:n_pieces]
    a0, b0, a1, b1, mids, slope0, slope1, nrm0, nrm1, hid0, hid1 = refs[n_pieces : n_pieces + 11]
    x_all, wide_n, wide_h, sems = refs[n_pieces + 11 :]
    collect(xs, x_all, sems)
    a_col, b_col = columns_of(place[1])

    def section(x, a, b, part, slope, nrm, hid):
        wide, factor, scaled = rows_norm(x)
        normed = scaled.astype(BF16)
        wide_n[...] = normed
        pre = dot(normed, a[...])
        sigma = jax.nn.sigmoid(pre)
        hidden = (pre * sigma).astype(BF16)
        wide_h[...] = hidden
        slope[part, :] = slope_of(pre).astype(slope.dtype)
        nrm[part, :] = wide_n[:, pl.ds(a_col, 128)]
        hid[part, :] = wide_h[:, pl.ds(b_col, 256)]
        if b is None:
            return None
        return (wide + dot(hidden, b[...])).astype(BF16)

    @pl.loop(0, x_all.shape[0] // chunk)
    def _(i):
        part = pl.ds(pl.multiple_of(i * chunk, chunk), chunk)
        mid = section(x_all[part, :], a0, b0, part, slope0, nrm0, hid0)
        mids[part, :] = mid
        section(mid, a1, None, part, slope1, nrm1, hid1)


def grad_kernel(n_pieces, chunk, place, *refs):
    gs = refs[:n_pieces]
    mids, slope0, slope1, nrm0, nrm1, hid0, hid1, b0t, a1t, b1t = refs[n_pieces : n_pieces + 10]
    leave, stay, leave_near, stay_near = refs[n_pieces + 10 : n_pieces + 14]
    g_all, acc_a0, acc_b0, acc_a1, acc_b1, sems = refs[n_pieces + 14 :]
    collect(gs, g_all, sems)
    replica, core = place[1], place[2]
    a_col, b_col = columns_of(replica)

    @pl.loop(0, g_all.shape[0] // chunk)
    def _(i):
        part = pl.ds(pl.multiple_of(i * chunk, chunk), chunk)
        g1 = g_all[part, :]
        wide1, factor1, scaled1 = rows_norm(mids[part, :])
        d_pre1 = (dot(g1, b1t[...]) * slope1[part, :].astype(F32)).astype(BF16)
        d_normed1 = dot(d_pre1, a1t[...])
        inner = jnp.mean(d_normed1 * scaled1, axis=-1, keepdims=True)
        g0 = (g1.astype(F32) + factor1 * (d_normed1 - scaled1 * inner)).astype(BF16)
        d_pre0 = (dot(g0, b0t[...]) * slope0[part, :].astype(F32)).astype(BF16)
        terms = (
            (acc_a0, dot_tn(nrm0[part, :], d_pre0)),
            (acc_a1, dot_tn(nrm1[part, :], d_pre1)),
            (acc_b0, dot_tn(hid0[part, :], g0)),
            (acc_b1, dot_tn(hid1[part, :], g1)),
        )
        for acc, term in terms:
            acc[...] = jnp.where(i == 0, term, acc[...] + term)

    d = g_all.shape[1]

    def write(target, acc_a, acc_b, slice_of):
        a_row = pl.multiple_of(lax.rem(slice_of, 4) * 32, 32)
        b_row = pl.multiple_of(slice_of * 96 - b_col, 32)
        count = acc_a.shape[1] // d
        for j in range(count):
            target[32 * j : 32 * (j + 1), :] = acc_a[
                pl.ds(a_row, 32), d * j : d * (j + 1)
            ].astype(target.dtype)
        target[32 * count : 32 * count + 96, :] = acc_b[pl.ds(b_row, 96), :].astype(target.dtype)

    near = replica + 1 - 2 * lax.rem(replica, 2)

    @pl.when(core == 0)
    def _():
        write(stay, acc_a0, acc_b0, replica)
        write(leave, acc_a1, acc_b1, replica)
        write(stay_near, acc_a0, acc_b0, near)
        write(leave_near, acc_a1, acc_b1, near)

    @pl.when(core == 1)
    def _():
        write(leave, acc_a0, acc_b0, replica)
        write(stay, acc_a1, acc_b1, replica)
        write(leave_near, acc_a0, acc_b0, near)
        write(stay_near, acc_a1, acc_b1, near)


def finish_kernel(first, second, third, fourth, grad_a, grad_b):
    total = first[...].astype(F32) + second[...].astype(F32)
    total = total + (third[...].astype(F32) + fourth[...].astype(F32))
    d = total.shape[1]
    count = grad_a.shape[1] // d
    for j in range(count):
        grad_a[:, d * j : d * (j + 1)] = total[32 * j : 32 * (j + 1), :]
    grad_b[...] = total[32 * count :, :]


def call(kernel, ins, outs, flops, scratch=(), limit=8, out_specs=None, aliases=None):
    return pl.pallas_call(
        kernel,
        out_shape=outs,
        in_specs=ins,
        out_specs=jax.tree.map(lambda _: VMEM, outs) if out_specs is None else out_specs,
        scratch_shapes=list(scratch),
        input_output_aliases=aliases or {},
        compiler_params=pltpu.CompilerParams(vmem_limit_bytes=limit * MIB),
        cost_estimate=pl.CostEstimate(flops=flops, bytes_accessed=MIB, transcendentals=0),
    )


def along(values, steps):
    n = lax.axis_size("dp")
    return [
        lax.ppermute(v, "dp", [(d, (d + 2 * k) % n) for d in range(n)])
        for v, k in zip(values, steps)
    ]


def gather_near(x):
    return along([x] * 4, (1, -1, 2, -2))


def gather_far(low, high):
    return along([low, high, low], (1, -1, 2))


def follow(arrays, *values):
    shapes = [jax.ShapeDtypeStruct(v.shape, v.dtype) for v in arrays]
    n = len(shapes)
    return call(
        functools.partial(follow_kernel, n),
        [VMEM] * (n + len(values)),
        shapes,
        FOLLOW_FLOPS,
        aliases={i: i for i in range(n)},
        limit=1,
    )(*arrays, *values)


FOLLOW_FLOPS = 4 * 10**9
TURN_WEIGHTS_AT = 2


def per_device(feed, proj_in, proj_out):
    sections = lax.axis_size("section")
    stages = sections // 2
    replicas = lax.axis_size("dp")
    position = lax.axis_index("section")
    replica = lax.axis_index("dp")
    core = lax.rem(position, 2)
    chip = lax.div(position, 2)
    stage = jnp.where(core == 0, chip, stages - 1 - chip)
    place = jnp.stack([stage, replica, core]).astype(jnp.int32)

    d, r = proj_in.shape[2:]
    micro, part = feed.shape[1:3]
    rows = micro * part
    total = rows * replicas // 2
    chunk = 512

    def bf(*shape):
        return jax.ShapeDtypeStruct(shape, BF16)

    def f32(*shape):
        return jax.ShapeDtypeStruct(shape, F32)

    place, feed, proj_in, proj_out = lax.optimization_barrier((place, feed, proj_in, proj_out))
    feed, proj_in, proj_out = (
        pltpu.with_memory_space_constraint(v, pltpu.HBM) for v in (feed, proj_in, proj_out)
    )
    a_send, b_send = call(
        offer_kernel,
        [SMEM, HBM, HBM],
        (bf(d, r), bf(r, d)),
        0,
        scratch=(pltpu.SemaphoreType.DMA((2,)),),
    )(place, proj_in, proj_out)
    swap = [(s, s ^ 1) for s in range(sections)]
    a1 = lax.ppermute(a_send, "section", swap)
    b1 = lax.ppermute(b_send, "section", swap)
    place_late, a_send = lax.optimization_barrier((place, a_send))
    x0, a0, b0 = call(
        load_kernel,
        [SMEM, HBM, HBM, HBM],
        (bf(micro, part, d), bf(d, r), bf(r, d)),
        FOLLOW_FLOPS,
        scratch=(pltpu.SemaphoreType.DMA((3,)),),
    )(place_late, feed, proj_in, proj_out)
    a1, b1 = call(
        land_kernel,
        [HBM, HBM],
        (bf(d, r), bf(r, d)),
        0,
        scratch=(pltpu.SemaphoreType.DMA((2,)),),
    )(a1, b1)
    weights = (a0, b0, a1, b1)
    step_flops = 8 * rows * d * r

    def hop(value, t, back=False):
        last = sections - 1
        pairs = [(2 * t, 2 * t + 2), (last - 2 * t, last - 2 * t - 2)]
        if back:
            pairs = [(b, a) for a, b in pairs]
        cycles = []
        for a, b in pairs:
            if (a, b) not in cycles:
                cycles += [(a, b), (b, b ^ 1), (b ^ 1, a ^ 1), (a ^ 1, a)]
        used = [a for a, _ in cycles]
        swaps = [(s, s ^ 1) for s in range(sections) if s not in used]
        return lax.ppermute(value, "section", cycles + swaps)

    xs = [x0.reshape(rows, d)]
    for t in range(stages - 1):
        y = call(
            functools.partial(forward_kernel, t), [SMEM] + [VMEM] * 5, bf(rows, d), step_flops
        )(place, xs[-1], *weights)
        came = hop(y, t)
        if t == TURN_WEIGHTS_AT:
            turned = call(
                turn_weights_kernel,
                [VMEM] * 5,
                (bf(r, d), bf(d, r), bf(r, d), bf(d, r)),
                FOLLOW_FLOPS,
            )(y, *weights)
            came, turned = lax.optimization_barrier((came, turned))
        xs.append(came)
    x, x_sent, mid, slope0, slope1, seed, back = call(
        turn_kernel,
        [SMEM] + [VMEM] * (stages + 8),
        (bf(rows, d),) * 3 + (f32(rows, r),) * 2 + (bf(rows, d),) * 2,
        2 * step_flops,
    )(place, *xs, *weights, *turned)

    gs = [seed]
    pieces, kept = [x], None
    for t in range(stages - 2, -1, -1):
        came = hop(back, t, True)
        if len(pieces) == 1:
            (x_sent,) = follow([x_sent], back)
            pieces += gather_near(x_sent)
        elif len(pieces) == 5:
            pieces += gather_far(*follow(pieces[3:], back, *pieces[1:3]))
        elif kept is None:
            kept = call(
                functools.partial(recompute_kernel, len(pieces), chunk),
                [SMEM] + [HBM] * len(pieces) + [VMEM] * 4,
                (
                    bf(total, d),
                    bf(total, r),
                    bf(total, r),
                    bf(total, 128),
                    bf(total, 128),
                    bf(total, 256),
                    bf(total, 256),
                ),
                6 * total * d * r,
                scratch=(
                    pltpu.VMEM((total, d), BF16),
                    pltpu.VMEM((chunk, d), BF16),
                    pltpu.VMEM((chunk, r), BF16),
                    pltpu.SemaphoreType.DMA((len(pieces),)),
                ),
                limit=20,
            )(place, *pieces, *weights)
            came, kept = lax.optimization_barrier((came, kept))
        gs.append(came)
        if t > 0:
            back = call(
                functools.partial(backward_kernel, t),
                [SMEM] + [VMEM] * 9,
                bf(rows, d),
                step_flops,
            )(place, came, x, mid, slope0, slope1, *turned)
    g = call(choose_kernel, [SMEM] + [VMEM] * stages, bf(rows, d), 0)(place, *gs[::-1])
    pieces = [g] + gather_near(g)
    pieces += gather_far(*pieces[3:])

    slab = (d * r + r * d) // replicas // d
    leave, stay, leave_near, stay_near = call(
        functools.partial(grad_kernel, len(pieces), chunk),
        [SMEM] + [HBM] * len(pieces) + [VMEM] * 10,
        (bf(slab, d),) * 4,
        10 * total * d * r,
        scratch=(
            pltpu.VMEM((total, d), BF16),
            pltpu.VMEM((128, r), F32),
            pltpu.VMEM((256, d), F32),
            pltpu.VMEM((128, r), F32),
            pltpu.VMEM((256, d), F32),
            pltpu.SemaphoreType.DMA((len(pieces),)),
        ),
        limit=20,
    )(place, *pieces, *kept, *turned[1:])
    cross = [(s, s + 1 if s % 2 == 0 else sections - 1 - s) for s in range(sections)]
    mirror = [(s, s if s % 2 == 0 else sections - s) for s in range(sections)]

    def send(value, targets, near):
        pairs = [
            (s * replicas + e, t * replicas + (e ^ near)) for s, t in targets for e in range(replicas)
        ]
        return lax.ppermute(value, ("section", "dp"), pairs)

    parts = [
        send(leave_near, cross, 1),
        send(stay_near, mirror, 1),
        send(leave, cross, 0),
        send(stay, mirror, 0),
    ]
    grad_a, grad_b = call(
        finish_kernel, [VMEM] * 4, (f32(d // replicas, r), f32(r // replicas, d)), 0
    )(*parts)
    return grad_a[None], grad_b[None]


def solution(mesh):
    in_specs = (
        P(None, None, "dp", None),
        P(None, "section", None, None),
        P(None, "section", None, None),
    )
    out_specs = (P("section", "dp", None), P("section", "dp", None))
    return jax.shard_map(
        per_device, mesh=mesh, in_specs=in_specs, out_specs=out_specs, check_vma=False
    )
```

```python
import functools

import jax
import jax.numpy as jnp
from jax import lax
from jax.experimental import pallas as pl
from jax.experimental.pallas import tpu as pltpu
from jax.sharding import PartitionSpec as P

F32 = jnp.float32
BF16 = jnp.bfloat16
SEED_SCALE = 8.0 / 1024.0
MIB = 1024 * 1024
VMEM = pl.BlockSpec(memory_space=pltpu.VMEM)
SMEM = pl.BlockSpec(memory_space=pltpu.SMEM)
HBM = pl.BlockSpec(memory_space=pltpu.HBM)


def dot(a, b):
    return jnp.dot(a, b, preferred_element_type=F32)


def dot_tn(a, b):
    return lax.dot_general(a, b, (((0,), (0,)), ((), ())), preferred_element_type=F32)


def rows_norm(x):
    wide = x.astype(F32)
    factor = lax.rsqrt(jnp.mean(wide * wide, axis=-1, keepdims=True) + 1e-05)
    return wide, factor, wide * factor


def section_forward(x, a, b):
    wide, factor, scaled = rows_norm(x)
    pre = dot(scaled.astype(BF16), a)
    hidden = (pre * jax.nn.sigmoid(pre)).astype(BF16)
    return (wide + dot(hidden, b)).astype(BF16), pre


def slope_of(pre):
    sigma = jax.nn.sigmoid(pre)
    return sigma * (1.0 + pre * (1.0 - sigma))


def section_backward(x, slope, a_t, b_t, g):
    wide, factor, scaled = rows_norm(x)
    d_pre = (dot(g, b_t) * slope).astype(BF16)
    d_normed = dot(d_pre, a_t)
    inner = jnp.mean(d_normed * scaled, axis=-1, keepdims=True)
    return (g.astype(F32) + factor * (d_normed - scaled * inner)).astype(BF16)


def forward_kernel(t, place, x, a0, b0, a1, b1, y):
    @pl.when(place[0] == t)
    def _():
        mid, _ = section_forward(x[...], a0[...], b0[...])
        y[...] = section_forward(mid, a1[...], b1[...])[0]


def turn_kernel(place, *refs):
    n = len(refs) - 15
    xs = refs[:n]
    a0, b0, a1, b1, a0t, b0t, a1t, b1t, x, x_sent, mid, slope0, slope1, seed, g_out = refs[n:]
    for t in range(n):

        @pl.when(place[0] == t)
        def _():
            x[...] = xs[t][...]
            x_sent[...] = xs[t][...]

    h, p0 = section_forward(x[...], a0[...], b0[...])
    mid[...] = h
    slope0[...] = slope_of(p0)
    y, p1 = section_forward(h, a1[...], b1[...])
    slope1[...] = slope_of(p1)

    @pl.when(place[0] == n - 1)
    def _():
        g = (SEED_SCALE * y.astype(F32)).astype(BF16)
        seed[...] = g
        half = section_backward(h, slope1[...], a1t[...], b1t[...], g)
        g_out[...] = section_backward(x[...], slope0[...], a0t[...], b0t[...], half)


def backward_kernel(t, place, g, x, mid, slope0, slope1, a0t, b0t, a1t, b1t, g_out):
    @pl.when(place[0] == t)
    def _():
        half = section_backward(mid[...], slope1[...], a1t[...], b1t[...], g[...])
        g_out[...] = section_backward(x[...], slope0[...], a0t[...], b0t[...], half)


def choose_kernel(place, *refs):
    gs, g = refs[:-1], refs[-1]
    for t, ref in enumerate(gs):

        @pl.when(place[0] == t)
        def _():
            g[...] = ref[...]


def follow_kernel(n, *refs):
    del n, refs


def copy_all(moves, sems):
    copies = [pltpu.make_async_copy(s, t, sems.at[i]) for i, (s, t) in enumerate(moves)]
    for copy in copies:
        copy.start()
    for copy in copies:
        copy.wait()


def offer_kernel(place, proj_in, proj_out, a_send, b_send, sems):
    other = 1 - place[2]
    copy_all(((proj_in.at[other, 0], a_send), (proj_out.at[other, 0], b_send)), sems)


def load_kernel(place, feed, proj_in, proj_out, x0, a0, b0, sems):
    own = place[2]
    copy_all(
        ((proj_in.at[own, 0], a0), (proj_out.at[own, 0], b0), (feed.at[own], x0)), sems
    )


def land_kernel(a_ref, b_ref, a1, b1, sems):
    copy_all(((a_ref, a1), (b_ref, b1)), sems)


def turn_weights_kernel(y, *refs):
    del y
    for source, target in zip(refs[:4], refs[4:]):
        step = 256

        @pl.loop(0, source.shape[0] // step)
        def _(i):
            part = pl.ds(pl.multiple_of(i * step, step), step)
            target[:, part] = source[part, :].T


def columns_of(replica):
    pair = replica // 2
    a_col = pl.multiple_of((pair // 2) * 128, 128)
    b_col = pl.multiple_of(((pair * 192) // 128) * 128, 128)
    return a_col, b_col


def collect(pieces, whole, sems):
    start, copies = 0, []
    for i, piece in enumerate(pieces):
        count = piece.shape[0]
        copies.append(
            pltpu.make_async_copy(piece, whole.at[pl.ds(start, count), :], sems.at[i])
        )
        start += count
    for copy in copies:
        copy.start()
    for copy in copies:
        copy.wait()


def recompute_kernel(n_pieces, chunk, place, *refs):
    xs = refs[:n_pieces]
    a0, b0, a1, b1, mids, slope0, slope1, nrm0, nrm1, hid0, hid1 = refs[n_pieces : n_pieces + 11]
    x_all, wide_n, wide_h, sems = refs[n_pieces + 11 :]
    collect(xs, x_all, sems)
    a_col, b_col = columns_of(place[1])

    def section(x, a, b, part, slope, nrm, hid):
        wide, factor, scaled = rows_norm(x)
        normed = scaled.astype(BF16)
        wide_n[...] = normed
        pre = dot(normed, a[...])
        sigma = jax.nn.sigmoid(pre)
        hidden = (pre * sigma).astype(BF16)
        wide_h[...] = hidden
        slope[part, :] = slope_of(pre).astype(slope.dtype)
        nrm[part, :] = wide_n[:, pl.ds(a_col, 128)]
        hid[part, :] = wide_h[:, pl.ds(b_col, 256)]
        if b is None:
            return None
        return (wide + dot(hidden, b[...])).astype(BF16)

    @pl.loop(0, x_all.shape[0] // chunk)
    def _(i):
        part = pl.ds(pl.multiple_of(i * chunk, chunk), chunk)
        mid = section(x_all[part, :], a0, b0, part, slope0, nrm0, hid0)
        mids[part, :] = mid
        section(mid, a1, None, part, slope1, nrm1, hid1)


def grad_kernel(n_pieces, chunk, place, *refs):
    gs = refs[:n_pieces]
    mids, slope0, slope1, nrm0, nrm1, hid0, hid1, b0t, a1t, b1t = refs[n_pieces : n_pieces + 10]
    leave, stay, leave_near, stay_near = refs[n_pieces + 10 : n_pieces + 14]
    g_all, acc_a0, acc_b0, acc_a1, acc_b1, sems = refs[n_pieces + 14 :]
    collect(gs, g_all, sems)
    replica, core = place[1], place[2]
    a_col, b_col = columns_of(replica)

    @pl.loop(0, g_all.shape[0] // chunk)
    def _(i):
        part = pl.ds(pl.multiple_of(i * chunk, chunk), chunk)
        g1 = g_all[part, :]
        wide1, factor1, scaled1 = rows_norm(mids[part, :])
        d_pre1 = (dot(g1, b1t[...]) * slope1[part, :].astype(F32)).astype(BF16)
        d_normed1 = dot(d_pre1, a1t[...])
        inner = jnp.mean(d_normed1 * scaled1, axis=-1, keepdims=True)
        g0 = (g1.astype(F32) + factor1 * (d_normed1 - scaled1 * inner)).astype(BF16)
        d_pre0 = (dot(g0, b0t[...]) * slope0[part, :].astype(F32)).astype(BF16)
        terms = (
            (acc_a0, dot_tn(nrm0[part, :], d_pre0)),
            (acc_a1, dot_tn(nrm1[part, :], d_pre1)),
            (acc_b0, dot_tn(hid0[part, :], g0)),
            (acc_b1, dot_tn(hid1[part, :], g1)),
        )
        for acc, term in terms:
            acc[...] = jnp.where(i == 0, term, acc[...] + term)

    d = g_all.shape[1]

    def write(target, acc_a, acc_b, slice_of):
        a_row = pl.multiple_of(lax.rem(slice_of, 4) * 32, 32)
        b_row = pl.multiple_of(slice_of * 96 - b_col, 32)
        count = acc_a.shape[1] // d
        for j in range(count):
            target[32 * j : 32 * (j + 1), :] = acc_a[
                pl.ds(a_row, 32), d * j : d * (j + 1)
            ].astype(target.dtype)
        target[32 * count : 32 * count + 96, :] = acc_b[pl.ds(b_row, 96), :].astype(target.dtype)

    near = replica + 1 - 2 * lax.rem(replica, 2)

    @pl.when(core == 0)
    def _():
        write(stay, acc_a0, acc_b0, replica)
        write(leave, acc_a1, acc_b1, replica)
        write(stay_near, acc_a0, acc_b0, near)
        write(leave_near, acc_a1, acc_b1, near)

    @pl.when(core == 1)
    def _():
        write(leave, acc_a0, acc_b0, replica)
        write(stay, acc_a1, acc_b1, replica)
        write(leave_near, acc_a0, acc_b0, near)
        write(stay_near, acc_a1, acc_b1, near)


def finish_kernel(first, second, third, fourth, grad_a, grad_b):
    total = first[...].astype(F32) + second[...].astype(F32)
    total = total + (third[...].astype(F32) + fourth[...].astype(F32))
    d = total.shape[1]
    count = grad_a.shape[1] // d
    for j in range(count):
        grad_a[:, d * j : d * (j + 1)] = total[32 * j : 32 * (j + 1), :]
    grad_b[...] = total[32 * count :, :]


def call(kernel, ins, outs, flops, scratch=(), limit=8, out_specs=None, aliases=None):
    return pl.pallas_call(
        kernel,
        out_shape=outs,
        in_specs=ins,
        out_specs=jax.tree.map(lambda _: VMEM, outs) if out_specs is None else out_specs,
        scratch_shapes=list(scratch),
        input_output_aliases=aliases or {},
        compiler_params=pltpu.CompilerParams(vmem_limit_bytes=limit * MIB),
        cost_estimate=pl.CostEstimate(flops=flops, bytes_accessed=MIB, transcendentals=0),
    )


def along(values, steps):
    n, sections = lax.axis_size("dp"), lax.axis_size("section")

    def pairs(k):
        return [
            (s * n + e, s * n + (e + (2 * k if s % 2 == 0 else -2 * k)) % n)
            for s in range(sections)
            for e in range(n)
        ]

    return [lax.ppermute(v, ("section", "dp"), pairs(k)) for v, k in zip(values, steps)]


def gather_near(x):
    return along([x] * 4, (1, -1, 2, -2))


def gather_far(low, high):
    return along([low, high, low], (1, -1, 2))


def follow(arrays, *values):
    shapes = [jax.ShapeDtypeStruct(v.shape, v.dtype) for v in arrays]
    n = len(shapes)
    return call(
        functools.partial(follow_kernel, n),
        [VMEM] * (n + len(values)),
        shapes,
        FOLLOW_FLOPS,
        aliases={i: i for i in range(n)},
        limit=1,
    )(*arrays, *values)


FOLLOW_FLOPS = 4 * 10**9
TURN_WEIGHTS_AT = 2


def per_device(feed, proj_in, proj_out):
    sections = lax.axis_size("section")
    stages = sections // 2
    replicas = lax.axis_size("dp")
    position = lax.axis_index("section")
    replica = lax.axis_index("dp")
    core = lax.rem(position, 2)
    chip = lax.div(position, 2)
    stage = jnp.where(core == 0, chip, stages - 1 - chip)
    place = jnp.stack([stage, replica, core]).astype(jnp.int32)

    d, r = proj_in.shape[2:]
    micro, part = feed.shape[1:3]
    rows = micro * part
    total = rows * replicas // 2
    chunk = 512

    def bf(*shape):
        return jax.ShapeDtypeStruct(shape, BF16)

    def f32(*shape):
        return jax.ShapeDtypeStruct(shape, F32)

    place, feed, proj_in, proj_out = lax.optimization_barrier((place, feed, proj_in, proj_out))
    feed, proj_in, proj_out = (
        pltpu.with_memory_space_constraint(v, pltpu.HBM) for v in (feed, proj_in, proj_out)
    )
    a_send, b_send = call(
        offer_kernel,
        [SMEM, HBM, HBM],
        (bf(d, r), bf(r, d)),
        0,
        scratch=(pltpu.SemaphoreType.DMA((2,)),),
    )(place, proj_in, proj_out)
    swap = [(s, s ^ 1) for s in range(sections)]
    a1 = lax.ppermute(a_send, "section", swap)
    b1 = lax.ppermute(b_send, "section", swap)
    place_late, a_send = lax.optimization_barrier((place, a_send))
    x0, a0, b0 = call(
        load_kernel,
        [SMEM, HBM, HBM, HBM],
        (bf(micro, part, d), bf(d, r), bf(r, d)),
        FOLLOW_FLOPS,
        scratch=(pltpu.SemaphoreType.DMA((3,)),),
    )(place_late, feed, proj_in, proj_out)
    a1, b1 = call(
        land_kernel,
        [HBM, HBM],
        (bf(d, r), bf(r, d)),
        0,
        scratch=(pltpu.SemaphoreType.DMA((2,)),),
    )(a1, b1)
    weights = (a0, b0, a1, b1)
    step_flops = 8 * rows * d * r

    def hop(value, t, back=False):
        last = sections - 1
        pairs = [(2 * t, 2 * t + 2), (last - 2 * t, last - 2 * t - 2)]
        if back:
            pairs = [(b, a) for a, b in pairs]
        cycles = []
        for a, b in pairs:
            if (a, b) not in cycles:
                cycles += [(a, b), (b, b ^ 1), (b ^ 1, a ^ 1), (a ^ 1, a)]
        used = [a for a, _ in cycles]
        swaps = [(s, s ^ 1) for s in range(sections) if s not in used]
        return lax.ppermute(value, "section", cycles + swaps)

    xs = [x0.reshape(rows, d)]
    for t in range(stages - 1):
        y = call(
            functools.partial(forward_kernel, t), [SMEM] + [VMEM] * 5, bf(rows, d), step_flops
        )(place, xs[-1], *weights)
        came = hop(y, t)
        if t == TURN_WEIGHTS_AT:
            turned = call(
                turn_weights_kernel,
                [VMEM] * 5,
                (bf(r, d), bf(d, r), bf(r, d), bf(d, r)),
                FOLLOW_FLOPS,
            )(y, *weights)
            came, turned = lax.optimization_barrier((came, turned))
        xs.append(came)
    x, x_sent, mid, slope0, slope1, seed, back = call(
        turn_kernel,
        [SMEM] + [VMEM] * (stages + 8),
        (bf(rows, d),) * 3 + (f32(rows, r),) * 2 + (bf(rows, d),) * 2,
        2 * step_flops,
    )(place, *xs, *weights, *turned)

    gs = [seed]
    pieces, kept = [x], None
    for t in range(stages - 2, -1, -1):
        came = hop(back, t, True)
        if len(pieces) == 1:
            (x_sent,) = follow([x_sent], back)
            pieces += gather_near(x_sent)
        elif len(pieces) == 5:
            pieces += gather_far(*follow(pieces[3:], back, *pieces[1:3]))
        elif kept is None:
            kept = call(
                functools.partial(recompute_kernel, len(pieces), chunk),
                [SMEM] + [HBM] * len(pieces) + [VMEM] * 4,
                (
                    bf(total, d),
                    bf(total, r),
                    bf(total, r),
                    bf(total, 128),
                    bf(total, 128),
                    bf(total, 256),
                    bf(total, 256),
                ),
                6 * total * d * r,
                scratch=(
                    pltpu.VMEM((total, d), BF16),
                    pltpu.VMEM((chunk, d), BF16),
                    pltpu.VMEM((chunk, r), BF16),
                    pltpu.SemaphoreType.DMA((len(pieces),)),
                ),
                limit=20,
            )(place, *pieces, *weights)
            came, kept = lax.optimization_barrier((came, kept))
        gs.append(came)
        if t > 0:
            back = call(
                functools.partial(backward_kernel, t),
                [SMEM] + [VMEM] * 9,
                bf(rows, d),
                step_flops,
            )(place, came, x, mid, slope0, slope1, *turned)
    g = call(choose_kernel, [SMEM] + [VMEM] * stages, bf(rows, d), 0)(place, *gs[::-1])
    pieces = [g] + gather_near(g)
    pieces += gather_far(*pieces[3:])

    slab = (d * r + r * d) // replicas // d
    leave, stay, leave_near, stay_near = call(
        functools.partial(grad_kernel, len(pieces), chunk),
        [SMEM] + [HBM] * len(pieces) + [VMEM] * 10,
        (bf(slab, d),) * 4,
        10 * total * d * r,
        scratch=(
            pltpu.VMEM((total, d), BF16),
            pltpu.VMEM((128, r), F32),
            pltpu.VMEM((256, d), F32),
            pltpu.VMEM((128, r), F32),
            pltpu.VMEM((256, d), F32),
            pltpu.SemaphoreType.DMA((len(pieces),)),
        ),
        limit=20,
    )(place, *pieces, *kept, *turned[1:])
    cross = [(s, s + 1 if s % 2 == 0 else sections - 1 - s) for s in range(sections)]
    mirror = [(s, s if s % 2 == 0 else sections - s) for s in range(sections)]

    def send(value, targets, near):
        pairs = [
            (s * replicas + e, t * replicas + (e ^ near)) for s, t in targets for e in range(replicas)
        ]
        return lax.ppermute(value, ("section", "dp"), pairs)

    parts = [
        send(leave_near, cross, 1),
        send(stay_near, mirror, 1),
        send(leave, cross, 0),
        send(stay, mirror, 0),
    ]
    grad_a, grad_b = call(
        finish_kernel, [VMEM] * 4, (f32(d // replicas, r), f32(r // replicas, d)), 0
    )(*parts)
    return grad_a[None], grad_b[None]


def solution(mesh):
    in_specs = (
        P(None, None, "dp", None),
        P(None, "section", None, None),
        P(None, "section", None, None),
    )
    out_specs = (P("section", "dp", None), P("section", "dp", None))
    return jax.shard_map(
        per_device, mesh=mesh, in_specs=in_specs, out_specs=out_specs, check_vma=False
    )
```
